256 devices in a mesh: hst: 4 (over x), chip: 64 (over z, y, core).
Axes of the slice: x: 4, y: 4, z: 8, core: 2. Of those that a mesh axis runs over, the one named last changes fastest.
Arguments:
- inputs: bfloat16 [262144, 4096], P(('hst', 'chip')), may hold values from -6 to 6, as said below
- out_grads: bfloat16 [262144, 1024], P(('hst', 'chip')), may hold values from -4 to 4, as said below
Outputs:
- weight_grad: float32 [4096, 1024], P(('hst', 'chip'))
The draws below stay inside these ranges and needn't reach their ends.
Inputs may be any that keep to these rules, and one draw needn't show every extreme that they name: `inputs`: whole numbers. `out_grads`: whole numbers.
All inputs are finite; a program needn't handle non-finite values. Where the reference program divides by a largest or mean magnitude, that divisor is 1e-20 or more.
Results may differ from the reference program's by a relative error of at most 0.0003.
Values may be sent and summed in bfloat16 or wider, within the bound.
A program may use at most 128 MiB of HBM per device.

```python
import jax
import jax.numpy as jnp
from jax import lax

KV = 1024
DIN = 4096
BLOCK = 128
NB = 8
TOK_DEV = 1024
TOKENS = 262144
N_CHIP = 64
DEVICES = 256


def draw_inputs(key, part):
    pair_key = jax.random.fold_in(key, 11)
    key = jax.random.fold_in(key, 1)
    values = jax.random.randint(key, (TOKENS, DIN), -3, 4)
    pairing = jax.random.permutation(pair_key, DEVICES)
    owner = pairing[jnp.arange(TOKENS, dtype=jnp.int32) // TOK_DEV]
    column_block = jnp.arange(DIN, dtype=jnp.int32) // (DIN // DEVICES)
    factor = jnp.where(owner[:, None] == column_block[None, :], 2, 1)
    return (values * factor).astype(jnp.bfloat16)


def draw_out_grads(key, part):
    key = jax.random.fold_in(key, 2)
    values = jax.random.randint(key, (TOKENS, KV), -4, 5)
    return values.astype(jnp.bfloat16)


def setup_inputs(seed: int = 0) -> dict:
    key_list = jax.random.split(jax.random.key(seed), 3)
    inputs = draw_inputs(jax.random.fold_in(key_list[2], 71), 0)
    out_grads = draw_out_grads(jax.random.fold_in(key_list[2], 71), 0)
    return {"inputs": inputs, "out_grads": out_grads}


powers_list = [2.0 ** k for k in range(31)]
doubled_list = [2.0 ** (k + 1) for k in range(31)]

def hadamard_table(length):
    index = jnp.arange(length, dtype=jnp.int32)
    common = jnp.bitwise_and(index[:, None], index[None, :])
    parity = jnp.zeros((length, length), jnp.int32)
    for bit_number in range(length.bit_length() - 1):
        parity = parity + jnp.bitwise_and(jnp.right_shift(common, bit_number), 1)
    return 1.0 - 2.0 * (parity % 2).astype(jnp.float32)

def block_scale(largest):
    powers = jnp.array(powers_list, dtype=largest.dtype)
    doubled = jnp.array(doubled_list, dtype=largest.dtype)
    picked = jnp.where(largest[..., None] >= powers, doubled, jnp.ones_like(doubled))
    return lax.optimization_barrier(jnp.max(picked, axis=-1)) / 128.0

def rotate_blocks(matrix, table):
    shaped = matrix.reshape(matrix.shape[0], -1, table.shape[0])
    turned = jnp.einsum('rbj,jk->rbk', shaped, table, precision=lax.Precision.HIGHEST)
    return turned.reshape(matrix.shape)

def quantize(matrix):
    shaped = matrix.reshape(matrix.shape[0], NB, BLOCK)
    scales = block_scale(lax.optimization_barrier(jnp.max(jnp.abs(shaped), axis=2)))
    codes = jnp.floor(shaped / scales[:, :, None] + 0.5).astype(jnp.bfloat16)
    return (codes, scales)

def dequantize(codes, scales):
    values = codes.astype(jnp.float32) * scales[:, :, None]
    return values.reshape(values.shape[0], NB * BLOCK)

def reference(inputs, out_grads):
    table = hadamard_table(BLOCK)
    hosts = inputs.shape[0] // (TOK_DEV * N_CHIP)
    input_blocks = inputs.reshape(hosts, N_CHIP, TOK_DEV, DIN)
    grad_blocks = out_grads.reshape(hosts, N_CHIP, TOK_DEV, KV)

    def per_host(total, pair):
        host_inputs, host_grads = pair

        def per_chip(partial_value, item):
            chip_inputs, chip_grads = item
            local = lax.dot_general(chip_inputs, chip_grads, (((0,), (0,)), ((), ())), preferred_element_type=jnp.float32)
            codes, scales = quantize(rotate_blocks(local, table))
            return (partial_value + dequantize(codes, scales), None)
        partial_value, unused = lax.scan(per_chip, jnp.zeros((DIN, KV), jnp.float32), (host_inputs, host_grads))
        codes, scales = quantize(partial_value)
        return (total + dequantize(codes, scales), None)
    total, unused = lax.scan(per_host, jnp.zeros((DIN, KV), jnp.float32), (input_blocks, grad_blocks))
    factor = 1.0 / (512.0 * jnp.sqrt(jnp.float32(TOKENS)))
    return rotate_blocks(total, table) * factor
```

```python
import functools
import math

import jax
import jax.numpy as jnp
from jax import lax
from jax.experimental import pallas as pl
from jax.experimental.pallas import tpu as pltpu
from jax.sharding import PartitionSpec as P

MESH = pl.DeviceIdType.MESH
F32 = jnp.float32
BF16 = jnp.bfloat16
BLOCK = 128
HALF = BLOCK // 2
NX, NZ, NY, NK = 4, 8, 4, 2
TILES = NX
WIDE = TILES * BLOCK
SPLIT = 48
TALL = BLOCK - SPLIT
CHAIN = ((0, 1, 3, 5, 7), (0, 2, 4, 6, 7))
QCHAIN = ((0, 1, 3), (0, 2, 3))


def signs(upper):
    i = lax.broadcasted_iota(jnp.int32, (BLOCK, BLOCK), 0)
    j = lax.broadcasted_iota(jnp.int32, (BLOCK, BLOCK), 1)
    t = i & j
    if not upper:
        t = t & (HALF - 1)
    t = t ^ (t >> 4)
    t = t ^ (t >> 2)
    t = t ^ (t >> 1)
    value = (1 - 2 * (t & 1)).astype(F32)
    if not upper:
        value = jnp.where((i & HALF) == (j & HALF), value, 0.0)
    return value


def scale_pair(largest, count):
    scale = jnp.full_like(largest, 1.0 / 128.0)
    inverse = jnp.full_like(largest, 128.0)
    for k in range(count):
        above = largest >= 2.0**k
        scale = jnp.where(above, 2.0 ** (k + 1) / 128.0, scale)
        inverse = jnp.where(above, 128.0 / 2.0 ** (k + 1), inverse)
    return scale, inverse


def rounded_halves(w_ref, put):
    tops = []
    for j in range(NY):
        u = w_ref[j * BLOCK : j * BLOCK + HALF]
        v = w_ref[j * BLOCK + HALF : (j + 1) * BLOCK]
        tops.append(jnp.max(jnp.abs(u) + jnp.abs(v), axis=0, keepdims=True))
    scale, inverse = scale_pair(jnp.concatenate(tops, axis=0), 22)
    for j in range(NY):
        s, inv = scale[j : j + 1], inverse[j : j + 1]
        u = w_ref[j * BLOCK : j * BLOCK + HALF] * inv
        v = w_ref[j * BLOCK + HALF : (j + 1) * BLOCK] * inv
        put(j, 0, jnp.floor(u + v + 0.5) * s)
        put(j, HALF, jnp.floor(u - v + 0.5) * s)


def kernel(
    factor, a_ref, g_ref, out_ref,
    abuf, gbuf, gt, w0, w1, S, CS, CR, RY0, RY1, RZ0, RZ1, RZ20, RZ21, RY20, RY21, XC, XR, OT, OB,
    a_sem, g_sem, sib_s, sib_r, y1_s, y1_r, z1_s, z1_r, z2_s, z2_r, y2_s, y2_r, x_s, x_r, f_s, f_r,
):
    x = lax.axis_index("hst")
    c = lax.axis_index("chip")
    z, y, k = c // 8, (c // 2) % 4, c % 2

    def dev(x_, z_, y_, k_):
        return (x_, (z_ * NY + y_) * NK + k_)

    sibling = dev(x, z, y, 1 - k)
    y_next = (dev(x, z, (y + 1) % 4, k), dev(x, z, (y + 3) % 4, k))
    z_next = (dev(x, (z + 1) % 8, y, k), dev(x, (z + 7) % 8, y, k))
    place = y * 2 + k

    def mate(d):
        return (x, z * 8 + (place + d) % 8)

    def host(r):
        return ((x + r) % 4, c)

    def g_copy():
        return pltpu.make_async_copy(g_ref, gbuf, g_sem)

    def a_copy(i, r):
        off = jnp.where(i % 2 == 0, 4 + i // 2, 3 - i // 2)
        start = (((x + r) % 4) * 8 + (z + off) % 8) * BLOCK
        return pltpu.make_async_copy(
            a_ref.at[:, pl.ds(pl.multiple_of(start, BLOCK), BLOCK)],
            abuf.at[i, :, pl.ds(r * BLOCK, BLOCK)],
            a_sem.at[i, r],
        )

    g_copy().start()

    def start_a(i, carry):
        for r in range(TILES):
            a_copy(i, r).start()
        return carry

    lax.fori_loop(0, 8, start_a, 0)

    barrier = pltpu.get_barrier_semaphore()
    friends = [z_next[0], z_next[1]] + [host(r) for r in range(1, 4)] + [mate(d) for d in range(1, 8)]
    for friend in friends:
        pl.semaphore_signal(barrier, inc=1, device_id=friend, device_id_type=MESH)

    def remote(src, dst, ss, rs, to):
        return pltpu.make_async_remote_copy(
            src_ref=src, dst_ref=dst, send_sem=ss, recv_sem=rs, device_id=to, device_id_type=MESH
        )

    def sib_copy(i):
        return remote(CS.at[i], CR.at[i], sib_s.at[i], sib_r.at[i], sibling)

    def half(d):
        return pl.ds(d * (WIDE // 2), WIDE // 2)

    low, high = pl.ds(0, SPLIT), pl.ds(SPLIT, TALL)

    def y1_copy(i, d, s):
        if s == 0:
            src, dst = S.at[i, 0, high, half(d)], RY0.at[d, i]
        else:
            src, dst = S.at[i, QCHAIN[d][1], high, :], RY1.at[d, i]
        return remote(src, dst, y1_s.at[d, s, i], y1_r.at[d, s, i], y_next[d])

    def z1_copy(d, s, u):
        qs = pl.ds(2 * u, 2)
        if s == 0:
            src, dst = S.at[0, qs, low, half(d)], RZ0.at[d, u]
        else:
            src, dst = S.at[CHAIN[d][s], qs, low, :], RZ1.at[d, s - 1, u]
        return remote(src, dst, z1_s.at[d, s, u], z1_r.at[d, s, u], z_next[d])

    def z2_copy(d, s):
        if s == 0:
            src, dst = S.at[0, 3, high, half(d)], RZ20.at[d]
        else:
            src, dst = S.at[CHAIN[d][s], 3, high, :], RZ21.at[d, s - 1]
        return remote(src, dst, z2_s.at[d, s], z2_r.at[d, s], z_next[d])

    def y2_copy(d, s):
        if s == 0:
            src, dst = S.at[7, 0, low, half(d)], RY20.at[d]
        else:
            src, dst = S.at[7, QCHAIN[d][1], low, :], RY21.at[d]
        return remote(src, dst, y2_s.at[d, s], y2_r.at[d, s], y_next[d])

    def x_copy(r):
        return remote(XC.at[r], XR.at[r], x_s.at[r], x_r.at[r], host(r))

    def f_copy(d):
        rows = pl.ds(pl.multiple_of(((place + d) % 8) * 16, 16), 16)
        columns = pl.ds(pl.multiple_of(place * BLOCK, BLOCK), BLOCK)
        return remote(OT.at[rows, :], OB.at[:, columns], f_s.at[d], f_r.at[d], mate(d))

    def y1_first(i):
        for d in range(2):
            y1_copy(i, d, 0).wait_recv()
            q = QCHAIN[d][1]
            S[i, q, high, half(d)] += RY0[d, i]
            y1_copy(i, d, 1).start()

    def y1_last(i):
        for d in range(2):
            y1_copy(i, d, 1).wait_recv()
        S[i, 3, high, :] += RY1[0, i] + RY1[1, i]

    def z1_take(d, s):
        for u in range(2):
            z1_copy(d, s, u).wait_recv()
            slot = CHAIN[d][s + 1]
            if s == 0:
                S[slot, pl.ds(2 * u, 2), low, half(d)] += RZ0[d, u]
            else:
                S[slot, pl.ds(2 * u, 2), low, :] += RZ1[d, s - 1, u]
            if s < 3:
                z1_copy(d, s + 1, u).start()

    def z2_take(d, s):
        z2_copy(d, s).wait_recv()
        slot = CHAIN[d][s + 1]
        if s == 0:
            S[slot, 3, high, half(d)] += RZ20[d]
        else:
            S[slot, 3, high, :] += RZ21[d, s - 1]
        if s < 3:
            z2_copy(d, s + 1).start()

    g_copy().wait()
    table = signs(False).astype(BF16)
    for h in range(2):
        for q, off in enumerate((2, 1, 3, 0)):
            block = ((y + off) % 4) * 2 + (1 - k if h == 0 else k)
            columns = pl.ds(pl.multiple_of(block * BLOCK, BLOCK), BLOCK)
            turned = lax.dot_general(
                table, gbuf[:, columns], (((1,), (1,)), ((), ())), preferred_element_type=F32
            )
            start = h * 512 + q * BLOCK
            gt[start : start + BLOCK, :] = turned.astype(BF16)

    pl.semaphore_wait(barrier, len(friends))

    def own(i):
        def put(j, r, value):
            S[i, j, r : r + HALF, :] = value

        rounded_halves(w1, put)

    def finish(i):
        sib_copy(i).wait_recv()
        for q in range(NY):
            S[i, q] += CR[i, q].astype(F32)
        for d in range(2):
            y1_copy(i, d, 0).start()

    def step(i, carry):
        for r in range(TILES):
            a_copy(i, r).wait()
        w0[...] = jnp.dot(gt[0:512, :], abuf[i], preferred_element_type=F32)
        own(jnp.maximum(i - 1, 0))

        @pl.when(i >= 1)
        def _():
            finish(i - 1)

        @pl.when(i == 1)
        def _():
            for u in range(2):
                for d in range(2):
                    z1_copy(d, 0, u).start()

        @pl.when(i == 5)
        def _():
            for d in range(2):
                z1_take(d, 0)

        w1[...] = jnp.dot(gt[512:1024, :], abuf[i], preferred_element_type=F32)

        def put(j, r, value):
            CS[i, j, r : r + HALF, :] = value.astype(BF16)

        rounded_halves(w0, put)
        sib_copy(i).start()
        return carry

    lax.fori_loop(0, 8, step, 0)
    own(7)
    finish(7)

    for i in range(0, 3):
        y1_first(i)
    for d in range(2):
        z1_take(d, 1)
    for i in range(3, 8):
        y1_first(i)
    y1_last(0)
    for d in range(2):
        z2_copy(d, 0).start()
    y1_last(1)
    for d in range(2):
        z1_take(d, 2)
    y1_last(2)
    for d in range(2):
        z2_take(d, 0)
    y1_last(3)
    y1_last(4)
    for d in range(2):
        z2_take(d, 1)
    for d in range(2):
        z1_take(d, 3)
    for d in range(2):
        y2_copy(d, 0).start()
    y1_last(5)
    for d in range(2):
        y2_copy(d, 0).wait_recv()
        S[7, QCHAIN[d][1], low, half(d)] += RY20[d]
        y2_copy(d, 1).start()
    y1_last(6)
    for d in range(2):
        z2_take(d, 2)
    y1_last(7)
    for d in range(2):
        y2_copy(d, 1).wait_recv()
    S[7, 3, low, :] += RY21[0] + RY21[1]
    for d in range(2):
        z2_take(d, 3)

    part = S[7, 3]
    scale, inverse = scale_pair(jnp.max(jnp.abs(part), axis=0, keepdims=True), 31)
    value = jnp.floor(part * inverse + 0.5) * scale
    for r in range(1, TILES):
        XC[r] = value[:, r * BLOCK : (r + 1) * BLOCK].astype(BF16)
        x_copy(r).start()
    total = value[:, :BLOCK]
    for r in range(1, TILES):
        x_copy(r).wait_recv()
        total = total + XR[r].astype(F32)

    result = jnp.dot(
        total.T, signs(True), preferred_element_type=F32, precision=lax.Precision.HIGHEST
    )
    OT[...] = result * factor
    for d in range(1, 8):
        f_copy(d).start()
    mine = pl.ds(pl.multiple_of(place * 16, 16), 16)
    columns = pl.ds(pl.multiple_of(place * BLOCK, BLOCK), BLOCK)
    OB[:, columns] = OT[mine, :]
    for d in range(1, 8):
        f_copy(d).wait_recv()
    out_ref[...] = OB[...]

    def drain(i, carry):
        sib_copy(i).wait_send()
        for d in range(2):
            for s in range(2):
                y1_copy(i, d, s).wait_send()
        return carry

    lax.fori_loop(0, 8, drain, 0)
    for d in range(2):
        for s in range(4):
            for u in range(2):
                z1_copy(d, s, u).wait_send()
            z2_copy(d, s).wait_send()
        for s in range(2):
            y2_copy(d, s).wait_send()
    for r in range(1, TILES):
        x_copy(r).wait_send()
    for d in range(1, 8):
        f_copy(d).wait_send()


def body(inputs, out_grads):
    tokens, din = inputs.shape
    width = out_grads.shape[1]
    everyone = lax.axis_size("hst") * lax.axis_size("chip")
    factor = 1.0 / (512.0 * math.sqrt(tokens * everyone))
    half_wide = WIDE // 2
    dma = pltpu.SemaphoreType.DMA
    return pl.pallas_call(
        functools.partial(kernel, factor),
        out_shape=jax.ShapeDtypeStruct((din // everyone, width), F32),
        in_specs=[pl.BlockSpec(memory_space=pl.ANY)] * 2,
        out_specs=pl.BlockSpec(memory_space=pltpu.VMEM),
        scratch_shapes=[
            pltpu.VMEM((8, tokens, WIDE), BF16),
            pltpu.VMEM((tokens, width), BF16),
            pltpu.VMEM((width, tokens), BF16),
            pltpu.VMEM((512, WIDE), F32),
            pltpu.VMEM((512, WIDE), F32),
            pltpu.VMEM((8, NY, BLOCK, WIDE), F32),
            pltpu.VMEM((8, NY, BLOCK, WIDE), BF16),
            pltpu.VMEM((8, NY, BLOCK, WIDE), BF16),
            pltpu.VMEM((2, 8, TALL, half_wide), F32),
            pltpu.VMEM((2, 8, TALL, WIDE), F32),
            pltpu.VMEM((2, 2, 2, SPLIT, half_wide), F32),
            pltpu.VMEM((2, 3, 2, 2, SPLIT, WIDE), F32),
            pltpu.VMEM((2, TALL, half_wide), F32),
            pltpu.VMEM((2, 3, TALL, WIDE), F32),
            pltpu.VMEM((2, SPLIT, half_wide), F32),
            pltpu.VMEM((2, SPLIT, WIDE), F32),
            pltpu.VMEM((TILES, BLOCK, BLOCK), BF16),
            pltpu.VMEM((TILES, BLOCK, BLOCK), BF16),
            pltpu.VMEM((BLOCK, BLOCK), F32),
            pltpu.VMEM((16, width), F32),
            dma((8, TILES)),
            dma,
            dma((8,)),
            dma((8,)),
            dma((2, 2, 8)),
            dma((2, 2, 8)),
            dma((2, 4, 2)),
            dma((2, 4, 2)),
            dma((2, 4)),
            dma((2, 4)),
            dma((2, 2)),
            dma((2, 2)),
            dma((TILES,)),
            dma((TILES,)),
            dma((8,)),
            dma((8,)),
        ],
        compiler_params=pltpu.CompilerParams(
            collective_id=0, has_side_effects=True, vmem_limit_bytes=60 * 2**20
        ),
        name="reduce_gradient",
    )(inputs, out_grads)


def solution(mesh):
    placed = (P(("hst", "chip"), None), P(("hst", "chip"), None))
    return jax.shard_map(
        body, mesh=mesh, in_specs=placed, out_specs=P(("hst", "chip"), None), check_vma=False
    )
```

```python
import functools
import math

import jax
import jax.numpy as jnp
from jax import lax
from jax.experimental import pallas as pl
from jax.experimental.pallas import tpu as pltpu
from jax.sharding import PartitionSpec as P

MESH = pl.DeviceIdType.MESH
F32 = jnp.float32
BF16 = jnp.bfloat16
BLOCK = 128
HALF = BLOCK // 2
NX, NZ, NY, NK = 4, 8, 4, 2
TILES = NX
WIDE = TILES * BLOCK
SPLIT = 48
TALL = BLOCK - SPLIT
CHAIN = ((0, 1, 3, 5, 7), (0, 2, 4, 6, 7))
LAG = 2
QCHAIN = ((0, 1, 3), (0, 2, 3))


STEP = 80.0
SPAN = 120.0
FAR = 2.0**22


def coded(number):
    size = jnp.abs(number)
    value = jnp.exp2(size - SPAN)
    return jnp.where(number < 0, -value, value).astype(BF16), size


def decoded(code, minus_unit):
    value = code.astype(F32)
    size = jnp.floor(jnp.log(jnp.abs(value)) * (STEP / math.log(2.0)) + (SPAN * STEP + 0.5))
    return size * jnp.where(value < 0, minus_unit, -minus_unit)


def signs(upper):
    i = lax.broadcasted_iota(jnp.int32, (BLOCK, BLOCK), 0)
    j = lax.broadcasted_iota(jnp.int32, (BLOCK, BLOCK), 1)
    t = i & j
    if not upper:
        t = t & (HALF - 1)
    t = t ^ (t >> 4)
    t = t ^ (t >> 2)
    t = t ^ (t >> 1)
    value = (1 - 2 * (t & 1)).astype(F32)
    if not upper:
        value = jnp.where((i & HALF) == (j & HALF), value, 0.0)
    return value


def scale_pair(largest, count):
    scale = jnp.full_like(largest, 1.0 / 128.0)
    inverse = jnp.full_like(largest, 128.0)
    for k in range(count):
        above = largest >= 2.0**k
        scale = jnp.where(above, 2.0 ** (k + 1) / 128.0, scale)
        inverse = jnp.where(above, 128.0 / 2.0 ** (k + 1), inverse)
    return scale, inverse


def rounded_halves(w_ref, put, units):
    tops = []
    for j in range(NY):
        u = w_ref[j * BLOCK : j * BLOCK + HALF]
        v = w_ref[j * BLOCK + HALF : (j + 1) * BLOCK]
        tops.append(jnp.max(jnp.abs(u) + jnp.abs(v), axis=0, keepdims=True))
    largest = jnp.concatenate(tops, axis=0)
    scale, inverse = scale_pair(largest, 22)
    used = largest >= 1.0
    minus = jnp.max(jnp.where(used, -scale, -FAR), axis=0, keepdims=True)
    finest = jnp.max(jnp.where(used, inverse, 1.0 / FAR), axis=0, keepdims=True)
    for h in range(TILES):
        units[h : h + 1, :] = minus[:, h * BLOCK : (h + 1) * BLOCK]
        units[8 + h : 9 + h, :] = finest[:, h * BLOCK : (h + 1) * BLOCK]
    for j in range(NY):
        s, inv = scale[j : j + 1], inverse[j : j + 1]
        u = w_ref[j * BLOCK : j * BLOCK + HALF] * inv
        v = w_ref[j * BLOCK + HALF : (j + 1) * BLOCK] * inv
        put(j, 0, jnp.floor(u + v + 0.5) * s)
        put(j, HALF, jnp.floor(u - v + 0.5) * s)


def kernel(
    factor, a_ref, g_ref, out_ref, bad_ref,
    abuf, gbuf, gt, w0, w1, S, CS, CR, EY0, RY0, EY1, RY1, EZ0, RZ0, EZ1, RZ1, EZ20, RZ20, EZ21, RZ21,
    EY20, RY20, EY21, RY21, XC, XR, FC, FR, UO, UT, UC, UY, UZ, FM,
    a_sem, g_sem, sib_r, y1_r, z1_r, z2_r, y2_r, x_r, f_r, out_sem,
):
    x = lax.axis_index("hst")
    c = lax.axis_index("chip")
    z, y, k = c // 8, (c // 2) % 4, c % 2

    def dev(x_, z_, y_, k_):
        return (x_, (z_ * NY + y_) * NK + k_)

    sibling = dev(x, z, y, 1 - k)
    y_next = (dev(x, z, (y + 1) % 4, k), dev(x, z, (y + 3) % 4, k))
    z_next = (dev(x, (z + 1) % 8, y, k), dev(x, (z + 7) % 8, y, k))
    place = y * 2 + k

    def owner(r, d):
        return ((x + r) % 4, z * 8 + (place + d) % 8)

    def along(d):
        return (x, ((z + d) % 8) * 8 + place)

    peers = [(r, d) for r in range(TILES) for d in range(8) if (r, d) != (0, 0)]

    def g_copy():
        return pltpu.make_async_copy(g_ref, gbuf, g_sem)

    def a_copy(i, r):
        off = jnp.where(i % 2 == 0, 4 + i // 2, 3 - i // 2)
        start = (((x + r) % 4) * 8 + (z + off) % 8) * BLOCK
        return pltpu.make_async_copy(
            a_ref.at[:, pl.ds(pl.multiple_of(start, BLOCK), BLOCK)],
            abuf.at[i, :, pl.ds(r * BLOCK, BLOCK)],
            a_sem.at[i],
        )

    g_copy().start()

    def start_a(i, carry):
        for r in range(TILES):
            a_copy(i, r).start()
        return carry

    lax.fori_loop(0, 8, start_a, 0)

    barrier = pltpu.get_barrier_semaphore()
    friends = [along(d) for d in range(1, 8)] + [owner(r, d) for r, d in peers]
    for friend in friends:
        pl.semaphore_signal(barrier, inc=1, device_id=friend, device_id_type=MESH)

    def remote(src, dst, ss, rs, to):
        return pltpu.make_async_remote_copy(
            src_ref=src, dst_ref=dst, send_sem=ss, recv_sem=rs, device_id=to, device_id_type=MESH
        )

    def sib_copy(i):
        return remote(CS.at[i], CR.at[i], out_sem.at[0], sib_r.at[i], sibling)

    def y1_copy(i, d, s):
        src, dst = (EY0, RY0) if s == 0 else (EY1, RY1)
        return remote(src.at[d, i], dst.at[d, i], out_sem.at[1 + s], y1_r.at[d, s, i], y_next[d])

    def z1_copy(d, s, u):
        if s == 0:
            src, dst = EZ0.at[d, u], RZ0.at[d, u]
        else:
            src, dst = EZ1.at[d, s - 1, u], RZ1.at[d, s - 1, u]
        return remote(src, dst, out_sem.at[3 + min(s, 1)], z1_r.at[d, s, u], z_next[d])

    def z2_copy(d, s):
        if s == 0:
            src, dst = EZ20.at[d], RZ20.at[d]
        else:
            src, dst = EZ21.at[d, s - 1], RZ21.at[d, s - 1]
        return remote(src, dst, out_sem.at[5 + min(s, 1)], z2_r.at[d, s], z_next[d])

    def y2_copy(d, s):
        src, dst = (EY20, RY20) if s == 0 else (EY21, RY21)
        return remote(src.at[d], dst.at[d], out_sem.at[7 + s], y2_r.at[d, s], y_next[d])

    def f_copy(d):
        return remote(FC, FR.at[d], out_sem.at[9], f_r, along(d))

    def x_copy(r, d):
        src = XC.at[r * 8 + (place + d) % 8]
        return remote(src, XR.at[r * 8 + d], out_sem.at[10], x_r, owner(r, d))

    def relay(count, row, items):
        def one(t, top):
            rows = pl.ds(pl.multiple_of(row + 16 * t, 16), 16)
            for i, q, h, arrivals, leaving in items:
                columns = slice(h * BLOCK, (h + 1) * BLOCK)
                v = S[i, q, rows, columns]
                for ref, base, stride, unit in arrivals:
                    v = v + decoded(ref[base + stride * t], unit[h : h + 1])
                if leaving is None:
                    S[i, q, rows, columns] = v
                else:
                    ref, base, stride, unit = leaving
                    code, size = coded(v * (unit[8 + h : 9 + h] * (1.0 / STEP)))
                    ref[base + stride * t] = code
                    top = jnp.maximum(top, size)
            return top

        FM[...] = lax.fori_loop(0, count, one, FM[...])

    TR, LR = TALL // 16, SPLIT // 16

    def unit_of(ref):
        return ref[ref.shape[0] - 1].astype(F32)

    def sign_unit(ref, unit):
        ref[ref.shape[0] - 1] = unit.astype(BF16)

    def y1_start(i):
        unit = UC[i]
        items = []
        for d in range(2):
            sign_unit(EY0.at[d, i], unit)
            items += [(i, 0, 2 * d + e, [], (EY0.at[d, i], e, 2, unit)) for e in range(2)]
        relay(TR, SPLIT, items)
        for d in range(2):
            y1_copy(i, d, 0).start()

    def y1_first(i):
        items = []
        for d in range(2):
            y1_copy(i, d, 0).wait_recv()
            came = unit_of(RY0.at[d, i])
            unit = jnp.maximum(UC[i], came)
            sign_unit(EY1.at[d, i], unit)
            for h in range(TILES):
                arrivals = [(RY0.at[d, i], h % 2, 2, came)] if h // 2 == d else []
                items.append((i, QCHAIN[d][1], h, arrivals, (EY1.at[d, i], h, TILES, unit)))
        relay(TR, SPLIT, items)
        for d in range(2):
            y1_copy(i, d, 1).start()

    def y1_last(i):
        units = []
        for d in range(2):
            y1_copy(i, d, 1).wait_recv()
            units.append(unit_of(RY1.at[d, i]))
        arrivals = [[(RY1.at[d, i], h, TILES, units[d]) for d in range(2)] for h in range(TILES)]
        relay(TR, SPLIT, [(i, 3, h, arrivals[h], None) for h in range(TILES)])
        UY[i] = jnp.maximum(UC[i], jnp.maximum(units[0], units[1]))

    def z1_start():
        unit = UC[0]
        for u in range(2):
            items = []
            for d in range(2):
                sign_unit(EZ0.at[d, u], unit)
                for q in range(2):
                    for e in range(2):
                        leaving = (EZ0.at[d, u], q * LR * 2 + e, 2, unit)
                        items.append((0, 2 * u + q, 2 * d + e, [], leaving))
            relay(LR, 0, items)
            for d in range(2):
                z1_copy(d, 0, u).start()

    def z1_take(s, u):
        for d in range(2):
            z1_copy(d, s, u).wait_recv()
            ref = RZ0.at[d, u] if s == 0 else RZ1.at[d, s - 1, u]
            slot = CHAIN[d][s + 1]
            came = unit_of(ref)
            unit = jnp.maximum(UZ[slot], came)
            items = []
            for q in range(2):
                for h in range(TILES):
                    base = q * LR * TILES + h
                    arrivals = [(ref, base, TILES, came)]
                    if s == 0:
                        arrivals = [(ref, q * LR * 2 + h % 2, 2, came)] if h // 2 == d else []
                    leaving = (EZ1.at[d, s, u], base, TILES, unit) if s < 3 else None
                    items.append((slot, 2 * u + q, h, arrivals, leaving))
            if s < 3:
                sign_unit(EZ1.at[d, s, u], unit)
                relay(LR, 0, items)
                z1_copy(d, s + 1, u).start()
            else:
                UZ[slot] = unit
                relay(LR, 0, items)

    def z2_start():
        unit = UY[0]
        items = []
        for d in range(2):
            sign_unit(EZ20.at[d], unit)
            items += [(0, 3, 2 * d + e, [], (EZ20.at[d], e, 2, unit)) for e in range(2)]
        relay(TR, SPLIT, items)
        for d in range(2):
            z2_copy(d, 0).start()

    def z2_take(s):
        for d in range(2):
            z2_copy(d, s).wait_recv()
            ref = RZ20.at[d] if s == 0 else RZ21.at[d, s - 1]
            slot = CHAIN[d][s + 1]
            came = unit_of(ref)
            unit = jnp.maximum(UY[slot], came)
            items = []
            for h in range(TILES):
                arrivals = [(ref, h, TILES, came)]
                if s == 0:
                    arrivals = [(ref, h % 2, 2, came)] if h // 2 == d else []
                items.append((slot, 3, h, arrivals, (EZ21.at[d, s], h, TILES, unit) if s < 3 else None))
            if s < 3:
                sign_unit(EZ21.at[d, s], unit)
            relay(TR, SPLIT, items)
            if s < 3:
                z2_copy(d, s + 1).start()

    def y2_start():
        unit = UZ[7]
        items = []
        for d in range(2):
            sign_unit(EY20.at[d], unit)
            items += [(7, 0, 2 * d + e, [], (EY20.at[d], e, 2, unit)) for e in range(2)]
        relay(LR, 0, items)
        for d in range(2):
            y2_copy(d, 0).start()

    def y2_first():
        items = []
        for d in range(2):
            y2_copy(d, 0).wait_recv()
            came = unit_of(RY20.at[d])
            unit = jnp.maximum(UZ[7], came)
            sign_unit(EY21.at[d], unit)
            for h in range(TILES):
                arrivals = [(RY20.at[d], h % 2, 2, came)] if h // 2 == d else []
                items.append((7, QCHAIN[d][1], h, arrivals, (EY21.at[d], h, TILES, unit)))
        relay(LR, 0, items)
        for d in range(2):
            y2_copy(d, 1).start()

    def y2_last():
        items = []
        units = []
        for d in range(2):
            y2_copy(d, 1).wait_recv()
            units.append(unit_of(RY21.at[d]))
        for h in range(TILES):
            items.append((7, 3, h, [(RY21.at[d], h, TILES, units[d]) for d in range(2)], None))
        relay(LR, 0, items)

    FM[...] = jnp.zeros_like(FM)
    UT[...] = jnp.zeros_like(UT)
    UO[...] = jnp.zeros_like(UO)

    g_copy().wait()
    table = signs(False).astype(BF16)
    for h in range(2):
        for q, off in enumerate((2, 1, 3, 0)):
            block = ((y + off) % 4) * 2 + (1 - k if h == 0 else k)
            columns = pl.ds(pl.multiple_of(block * BLOCK, BLOCK), BLOCK)
            turned = lax.dot_general(
                table, gbuf[:, columns], (((1,), (1,)), ((), ())), preferred_element_type=F32
            )
            start = h * 512 + q * BLOCK
            gt[start : start + BLOCK, :] = turned.astype(BF16)

    def own(i):
        def put(j, r, value):
            S[i, j, r : r + HALF, :] = value

        rounded_halves(w1, put, UO.at[i])

    def finish(i):
        sib_copy(i).wait_recv()

        def add(t, carry):
            rows = pl.ds(pl.multiple_of(16 * t, 16), 16)
            for q in range(NY):
                for h in range(TILES):
                    columns = slice(h * BLOCK, (h + 1) * BLOCK)
                    S[i, q, rows, columns] += CR[i, (q * TILES + h) * 8 + t].astype(F32)
            return carry

        lax.fori_loop(0, 8, add, 0)
        unit = jnp.maximum(UO[i], unit_of(CR.at[i]))
        UC[i] = unit
        UZ[i] = unit
        y1_start(i)

    def multiply(i):
        pltpu.make_async_copy(a_ref.at[:, pl.ds(0, WIDE)], abuf.at[i], a_sem.at[i]).wait()
        w0[...] = jnp.dot(gt[0:512, :], abuf[i], preferred_element_type=F32)
        own(jnp.maximum(i - 1, 0))

    def multiply_more(i):
        w1[...] = jnp.dot(gt[512:1024, :], abuf[i], preferred_element_type=F32)

        def put(j, r, value):
            for h in range(TILES):
                for t in range(HALF // 16):
                    tile = value[t * 16 : (t + 1) * 16, h * BLOCK : (h + 1) * BLOCK]
                    CS[i, (j * TILES + h) * 8 + r // 16 + t] = tile.astype(BF16)

        rounded_halves(w0, put, UT)
        CS[i, NY * TILES * 8] = UT[...].astype(BF16)

    def step(i, carry):
        multiply(i)

        @pl.when(i >= LAG)
        def _():
            finish(i - LAG)

        @pl.when(i == LAG)
        def _():
            z1_start()

        @pl.when(i >= LAG + 2)
        def _():
            y1_first(i - LAG - 2)

        @pl.when(i == LAG + 4)
        def _():
            for u in range(2):
                z1_take(0, u)

        multiply_more(i)
        sib_copy(i).start()
        return carry

    multiply(0)
    multiply_more(0)
    pl.semaphore_wait(barrier, len(friends))
    sib_copy(0).start()
    lax.fori_loop(1, 8, step, 0)
    own(7)
    z1_take(1, 0)
    y1_last(0)
    z2_start()
    finish(6)
    z1_take(1, 1)
    y1_first(4)
    y1_last(1)
    finish(7)
    y1_first(5)
    y1_last(2)
    z2_take(0)
    z1_take(2, 0)
    y1_first(6)
    y1_last(3)
    z1_take(2, 1)
    y1_first(7)
    y1_last(4)
    z2_take(1)
    z1_take(3, 0)
    y1_last(5)
    z1_take(3, 1)
    y2_start()
    y1_last(6)
    z2_take(2)
    y2_first()
    FC[...] = FM[...]
    for d in range(1, 8):
        f_copy(d).start()
    y1_last(7)
    z2_take(3)
    y2_last()

    part = S[7, 3]
    scale, inverse = scale_pair(jnp.max(jnp.abs(part), axis=0, keepdims=True), 31)
    value = (jnp.floor(part * inverse + 0.5) * scale).T
    top = FM[...]
    remote(FR.at[pl.ds(1, 7)], FR.at[pl.ds(1, 7)], out_sem.at[9], f_r, sibling).wait_recv()
    for d in range(1, 8):
        top = jnp.maximum(top, FR[d])
    bad = jnp.where(top <= 2 * SPAN, 0.0, 1.0).astype(BF16)
    for r in range(TILES):
        for g in range(8):
            start = r * BLOCK + g * 16
            XC[r * 8 + g, 0:16] = value[start : start + 16].astype(BF16)
            XC[r * 8 + g, 16:32] = bad
    for r, d in peers:
        x_copy(r, d).start()
    XR[0] = XC[place]

    gone = (CS, EY0, EY1, EZ0, EZ1, EZ20, EZ21, EY20, EY21, FR.at[pl.ds(1, 7)])
    for n, ref in enumerate(gone):
        remote(ref, ref, out_sem.at[n], x_r, sibling).wait_send()

    remaining = pl.ds(1, TILES * 8 - 1)
    remote(XR.at[remaining], XR.at[remaining], out_sem.at[10], x_r, sibling).wait_recv()
    total = XR[0:8, 0:16].astype(F32)
    for r in range(1, TILES):
        total = total + XR[r * 8 : r * 8 + 8, 0:16].astype(F32)
    flags = XR[:, 16:32].astype(F32).reshape(TILES * 8 * 16, BLOCK)
    bad_ref[...] = jnp.full_like(bad_ref, jnp.max(flags))
    result = jnp.dot(
        total.reshape(BLOCK, BLOCK), signs(True),
        preferred_element_type=F32, precision=lax.Precision.HIGHEST,
    ) * factor
    for d in range(8):
        columns = pl.ds(pl.multiple_of(((place + 8 - d) % 8) * BLOCK, BLOCK), BLOCK)
        out_ref[:, columns] = result[d * 16 : (d + 1) * 16]
    remote(XR.at[remaining], XR.at[remaining], out_sem.at[10], x_r, sibling).wait_send()


def quick(inputs, out_grads):
    tokens, din = inputs.shape
    width = out_grads.shape[1]
    everyone = lax.axis_size("hst") * lax.axis_size("chip")
    factor = 1.0 / (512.0 * math.sqrt(tokens * everyone))
    tall, low = TALL // 16 * TILES, SPLIT // 16 * TILES
    dma = pltpu.SemaphoreType.DMA

    def tiles(*shape):
        return [pltpu.VMEM(shape + (16, BLOCK), BF16)]

    def both(*shape):
        return tiles(*shape) * 2

    unit = pltpu.VMEM((8, 16, BLOCK), F32)
    return pl.pallas_call(
        functools.partial(kernel, factor),
        out_shape=(
            jax.ShapeDtypeStruct((din // everyone, width), F32),
            jax.ShapeDtypeStruct((8, BLOCK), F32),
        ),
        in_specs=[pl.BlockSpec(memory_space=pl.ANY)] * 2,
        out_specs=[pl.BlockSpec(memory_space=pltpu.VMEM)] * 2,
        scratch_shapes=[
            pltpu.VMEM((8, tokens, WIDE), BF16),
            pltpu.VMEM((tokens, width), BF16),
            pltpu.VMEM((width, tokens), BF16),
            pltpu.VMEM((512, WIDE), F32),
            pltpu.VMEM((512, WIDE), F32),
            pltpu.VMEM((8, NY, BLOCK, WIDE), F32),
        ]
        + both(8, NY * TILES * 8 + 1)
        + both(2, 8, tall // 2 + 1)
        + both(2, 8, tall + 1)
        + both(2, 2, low + 1)
        + both(2, 3, 2, 2 * low + 1)
        + both(2, tall // 2 + 1)
        + both(2, 3, tall + 1)
        + both(2, low // 2 + 1)
        + both(2, low + 1)
        + [
            pltpu.VMEM((TILES * 8, 32, BLOCK), BF16),
            pltpu.VMEM((TILES * 8, 32, BLOCK), BF16),
            pltpu.VMEM((16, BLOCK), F32),
            pltpu.VMEM((8, 16, BLOCK), F32),
            unit,
            pltpu.VMEM((16, BLOCK), F32),
            unit,
            unit,
            unit,
            pltpu.VMEM((16, BLOCK), F32),
        ]
        + [dma((8,)), dma, dma((8,)), dma((2, 2, 8)), dma((2, 4, 2)), dma((2, 4)), dma((2, 2))]
        + [dma, dma, dma((11,))],
        compiler_params=pltpu.CompilerParams(
            collective_id=0, has_side_effects=True, vmem_limit_bytes=60 * 2**20
        ),
        name="reduce_gradient",
    )(inputs, out_grads)


powers_list = [2.0**k for k in range(31)]
doubled_list = [2.0 ** (k + 1) for k in range(31)]


def hadamard_table(length):
    index = jnp.arange(length, dtype=jnp.int32)
    common = jnp.bitwise_and(index[:, None], index[None, :])
    parity = jnp.zeros((length, length), jnp.int32)
    for bit_number in range(length.bit_length() - 1):
        parity = parity + jnp.bitwise_and(jnp.right_shift(common, bit_number), 1)
    return 1.0 - 2.0 * (parity % 2).astype(jnp.float32)


def block_scale(largest):
    powers = jnp.array(powers_list, dtype=jnp.float32)
    doubled = jnp.array(doubled_list, dtype=jnp.float32)
    picked = jnp.where(largest[..., None] >= powers, doubled, jnp.ones_like(doubled))
    return jnp.max(picked, axis=-1) / 128.0


def quantize_last(values):
    scales = block_scale(jnp.max(jnp.abs(values), axis=-1))
    codes = jnp.floor(values / scales[..., None] + 0.5).astype(jnp.bfloat16)
    return (codes, scales)


def dequantize_last(codes, scales):
    return codes.astype(jnp.float32) * scales[..., None]


def plain(inputs, out_grads):
    table = hadamard_table(BLOCK)
    hosts = lax.axis_size("hst")
    chips = lax.axis_size("chip")
    din = inputs.shape[1]
    width = out_grads.shape[1]
    blocks = width // BLOCK
    rows = din // (hosts * chips)
    token_count = inputs.shape[0] * hosts * chips
    local = lax.dot_general(
        inputs, out_grads, (((0,), (0,)), ((), ())), preferred_element_type=jnp.float32
    )
    rotated = jnp.einsum(
        "dbj,jk->dbk", local.reshape(din, blocks, BLOCK), table, precision=lax.Precision.HIGHEST
    )
    codes, scales = quantize_last(rotated)
    codes = codes.reshape(hosts, chips, rows, width)
    scales = scales.reshape(hosts, chips, rows, blocks)
    got_codes, got_scales = (
        lax.all_to_all(codes, "chip", split_axis=1, concat_axis=1, tiled=True),
        lax.all_to_all(
            scales.astype(jnp.bfloat16), "chip", split_axis=1, concat_axis=1, tiled=True
        ).astype(scales.dtype),
    )
    count = got_codes.shape[0]
    shaped = got_codes.reshape(count, chips, rows, blocks, BLOCK)
    partial_value = jnp.sum(dequantize_last(shaped, got_scales), axis=1)
    count = partial_value.shape[0]
    new_codes, new_scales = quantize_last(partial_value)
    codes2 = new_codes.reshape(count, rows, width)
    own_codes, own_scales = (
        lax.all_to_all(codes2, "hst", split_axis=0, concat_axis=0, tiled=True),
        lax.all_to_all(
            new_scales.astype(jnp.bfloat16), "hst", split_axis=0, concat_axis=0, tiled=True
        ).astype(new_scales.dtype),
    )
    shaped = own_codes.reshape(hosts, rows, blocks, BLOCK)
    total = jnp.sum(dequantize_last(shaped, own_scales), axis=0)
    result = jnp.einsum("rbj,jk->rbk", total, table, precision=lax.Precision.HIGHEST)
    factor = 1.0 / (512.0 * jnp.sqrt(jnp.float32(token_count)))
    return result.reshape(rows, width) * factor


def body(inputs, out_grads):
    result, bad = quick(inputs, out_grads)
    return lax.cond(bad[0, 0] > 0, plain, lambda a, b: result, inputs, out_grads)


def solution(mesh):
    placed = (P(("hst", "chip"), None), P(("hst", "chip"), None))
    return jax.shard_map(
        body, mesh=mesh, in_specs=placed, out_specs=P(("hst", "chip"), None), check_vma=False
    )
```

```python
import functools
import math

import jax
import jax.numpy as jnp
from jax import lax
from jax.experimental import pallas as pl
from jax.experimental.pallas import tpu as pltpu
from jax.sharding import PartitionSpec as P

MESH = pl.DeviceIdType.MESH
F32 = jnp.float32
BF16 = jnp.bfloat16
BLOCK = 128
HALF = BLOCK // 2
NX, NZ, NY, NK = 4, 8, 4, 2
TILES = NX
WIDE = TILES * BLOCK
SPLIT = 48
TALL = BLOCK - SPLIT
CHAIN = ((0, 1, 3, 5, 7), (0, 2, 4, 6, 7))
LAG = 3
QCHAIN = ((0, 1, 3), (0, 2, 3))


STEP = 80.0
SPAN = 120.0
FAR = 2.0**22


def coded(number):
    size = jnp.abs(number)
    value = jnp.exp2(size - SPAN)
    return jnp.where(number < 0, -value, value).astype(BF16), size


def decoded(code, minus_unit):
    value = code.astype(F32)
    size = jnp.floor(jnp.log(jnp.abs(value)) * (STEP / math.log(2.0)) + (SPAN * STEP + 0.5))
    return size * jnp.where(value < 0, minus_unit, -minus_unit)


def signs(upper):
    i = lax.broadcasted_iota(jnp.int32, (BLOCK, BLOCK), 0)
    j = lax.broadcasted_iota(jnp.int32, (BLOCK, BLOCK), 1)
    t = i & j
    if not upper:
        t = t & (HALF - 1)
    t = t ^ (t >> 4)
    t = t ^ (t >> 2)
    t = t ^ (t >> 1)
    value = (1 - 2 * (t & 1)).astype(F32)
    if not upper:
        value = jnp.where((i & HALF) == (j & HALF), value, 0.0)
    return value


def scale_pair(largest, count):
    scale = jnp.full_like(largest, 1.0 / 128.0)
    inverse = jnp.full_like(largest, 128.0)
    for k in range(count):
        above = largest >= 2.0**k
        scale = jnp.where(above, 2.0 ** (k + 1) / 128.0, scale)
        inverse = jnp.where(above, 128.0 / 2.0 ** (k + 1), inverse)
    return scale, inverse


def rounded_halves(w_ref, put, units):
    tops = []
    for j in range(NY):
        u = w_ref[j * BLOCK : j * BLOCK + HALF]
        v = w_ref[j * BLOCK + HALF : (j + 1) * BLOCK]
        tops.append(jnp.max(jnp.abs(u) + jnp.abs(v), axis=0, keepdims=True))
    largest = jnp.concatenate(tops, axis=0)
    scale, inverse = scale_pair(largest, 22)
    used = largest >= 1.0
    minus = jnp.max(jnp.where(used, -scale, -FAR), axis=0, keepdims=True)
    finest = jnp.max(jnp.where(used, inverse, 1.0 / FAR), axis=0, keepdims=True)
    for h in range(TILES):
        units[h : h + 1, :] = minus[:, h * BLOCK : (h + 1) * BLOCK]
        units[8 + h : 9 + h, :] = finest[:, h * BLOCK : (h + 1) * BLOCK]
    for j in range(NY):
        s, inv = scale[j : j + 1], inverse[j : j + 1]
        u = w_ref[j * BLOCK : j * BLOCK + HALF] * inv
        v = w_ref[j * BLOCK + HALF : (j + 1) * BLOCK] * inv
        put(j, 0, jnp.floor(u + v + 0.5) * s)
        put(j, HALF, jnp.floor(u - v + 0.5) * s)


def kernel(
    factor, a_ref, g_ref, out_ref, bad_ref,
    abuf, gbuf, gt, w0, w1, S, CS, CR, EY0, RY0, EY1, RY1, EZ0, RZ0, EZ1, RZ1, EZ20, RZ20, EZ21, RZ21,
    EY20, RY20, EY21, RY21, XC, XR, FC, FR, UO, UT, UC, UY, UZ, FM,
    a_sem, g_sem, sib_r, y1_r, z1_r, z2_r, y2_r, x_r, f_r, out_sem,
):
    x = lax.axis_index("hst")
    c = lax.axis_index("chip")
    z, y, k = c // 8, (c // 2) % 4, c % 2

    def dev(x_, z_, y_, k_):
        return (x_, (z_ * NY + y_) * NK + k_)

    sibling = dev(x, z, y, 1 - k)
    y_next = (dev(x, z, (y + 1) % 4, k), dev(x, z, (y + 3) % 4, k))
    z_next = (dev(x, (z + 1) % 8, y, k), dev(x, (z + 7) % 8, y, k))
    place = y * 2 + k

    def owner(r, d):
        return ((x + r) % 4, z * 8 + (place + d) % 8)

    def along(d):
        return (x, ((z + d) % 8) * 8 + place)

    peers = [(r, d) for r in range(TILES) for d in range(8) if (r, d) != (0, 0)]
    peers.sort(key=lambda p: -2 * min(p[0], TILES - p[0]) - min(p[1], 8 - p[1]))

    def kv_columns(h, q):
        block = ((y + (2, 1, 3, 0)[q]) % 4) * 2 + (1 - k if h == 0 else k)
        return pl.ds(pl.multiple_of(block * BLOCK, BLOCK), BLOCK)

    def g_copy(h, q):
        start = h * 512 + q * BLOCK
        return pltpu.make_async_copy(
            g_ref.at[:, kv_columns(h, q)], gbuf.at[:, pl.ds(start, BLOCK)], g_sem.at[h]
        )

    def a_copy(i, r):
        off = jnp.where(i % 2 == 0, 4 + i // 2, 3 - i // 2)
        start = (((x + r) % 4) * 8 + (z + off) % 8) * BLOCK
        return pltpu.make_async_copy(
            a_ref.at[:, pl.ds(pl.multiple_of(start, BLOCK), BLOCK)],
            abuf.at[i, :, pl.ds(r * BLOCK, BLOCK)],
            a_sem.at[i],
        )

    def start_a(i, carry):
        for r in range(TILES):
            a_copy(i, r).start()
        return carry

    for q in range(NY):
        g_copy(0, q).start()
    start_a(0, 0)

    barrier = pltpu.get_barrier_semaphore()
    friends = [along(d) for d in range(1, 8)] + [owner(r, d) for r, d in peers]
    for friend in friends:
        pl.semaphore_signal(barrier, inc=1, device_id=friend, device_id_type=MESH)

    def remote(src, dst, ss, rs, to):
        return pltpu.make_async_remote_copy(
            src_ref=src, dst_ref=dst, send_sem=ss, recv_sem=rs, device_id=to, device_id_type=MESH
        )

    def sib_copy(i):
        return remote(CS.at[i], CR.at[i], out_sem.at[0], sib_r.at[i], sibling)

    def y1_copy(i, d, s):
        src, dst = (EY0, RY0) if s == 0 else (EY1, RY1)
        return remote(src.at[d, i], dst.at[d, i], out_sem.at[1 + s], y1_r.at[d, s, i], y_next[d])

    def z1_copy(d, s, u):
        if s == 0:
            src, dst = EZ0.at[d, u], RZ0.at[d, u]
        else:
            src, dst = EZ1.at[d, s - 1, u], RZ1.at[d, s - 1, u]
        return remote(src, dst, out_sem.at[3 + min(s, 1)], z1_r.at[d, s, u], z_next[d])

    def z2_copy(d, s):
        if s == 0:
            src, dst = EZ20.at[d], RZ20.at[d]
        else:
            src, dst = EZ21.at[d, s - 1], RZ21.at[d, s - 1]
        return remote(src, dst, out_sem.at[5 + min(s, 1)], z2_r.at[d, s], z_next[d])

    def y2_copy(d, s):
        src, dst = (EY20, RY20) if s == 0 else (EY21, RY21)
        return remote(src.at[d], dst.at[d], out_sem.at[7 + s], y2_r.at[d, s], y_next[d])

    def f_copy(d):
        return remote(FC, FR.at[d], out_sem.at[9], f_r, along(d))

    def x_copy(r, d):
        src = XC.at[r * 8 + (place + d) % 8]
        return remote(src, XR.at[r * 8 + d], out_sem.at[10], x_r, owner(r, d))

    def relay(count, row, items):
        def one(t, top):
            rows = pl.ds(pl.multiple_of(row + 16 * t, 16), 16)
            for i, q, h, arrivals, leaving in items:
                columns = slice(h * BLOCK, (h + 1) * BLOCK)
                v = S[i, q, rows, columns]
                for ref, base, stride, unit in arrivals:
                    v = v + decoded(ref[base + stride * t], unit[h : h + 1])
                if leaving is None:
                    S[i, q, rows, columns] = v
                else:
                    ref, base, stride, unit = leaving
                    code, size = coded(v * (unit[8 + h : 9 + h] * (1.0 / STEP)))
                    ref[base + stride * t] = code
                    top = jnp.maximum(top, size)
            return top

        FM[...] = lax.fori_loop(0, count, one, FM[...], unroll=True)

    TR, LR = TALL // 16, SPLIT // 16

    def unit_of(ref):
        return ref[ref.shape[0] - 1].astype(F32)

    def sign_unit(ref, unit):
        ref[ref.shape[0] - 1] = unit.astype(BF16)

    def y1_first(i):
        items = []
        for d in range(2):
            y1_copy(i, d, 0).wait_recv()
            came = unit_of(RY0.at[d, i])
            unit = jnp.maximum(UC[i], came)
            sign_unit(EY1.at[d, i], unit)
            for h in range(TILES):
                arrivals = [(RY0.at[d, i], h % 2, 2, came)] if h // 2 == d else []
                items.append((i, QCHAIN[d][1], h, arrivals, (EY1.at[d, i], h, TILES, unit)))
        relay(TR, SPLIT, items)
        for d in range(2):
            y1_copy(i, d, 1).start()

    def y1_last(i):
        units = []
        for d in range(2):
            y1_copy(i, d, 1).wait_recv()
            units.append(unit_of(RY1.at[d, i]))
        arrivals = [[(RY1.at[d, i], h, TILES, units[d]) for d in range(2)] for h in range(TILES)]
        relay(TR, SPLIT, [(i, 3, h, arrivals[h], None) for h in range(TILES)])
        UY[i] = jnp.maximum(UC[i], jnp.maximum(units[0], units[1]))

    def z1_start():
        unit = UC[0]
        for u in range(2):
            items = []
            for d in range(2):
                sign_unit(EZ0.at[d, u], unit)
                for q in range(2):
                    for e in range(2):
                        leaving = (EZ0.at[d, u], q * LR * 2 + e, 2, unit)
                        items.append((0, 2 * u + q, 2 * d + e, [], leaving))
            relay(LR, 0, items)
            for d in range(2):
                z1_copy(d, 0, u).start()

    def z1_take(s, u):
        for d in range(2):
            z1_copy(d, s, u).wait_recv()
            ref = RZ0.at[d, u] if s == 0 else RZ1.at[d, s - 1, u]
            slot = CHAIN[d][s + 1]
            came = unit_of(ref)
            unit = jnp.maximum(UZ[slot], came)
            items = []
            for q in range(2):
                for h in range(TILES):
                    base = q * LR * TILES + h
                    arrivals = [(ref, base, TILES, came)]
                    if s == 0:
                        arrivals = [(ref, q * LR * 2 + h % 2, 2, came)] if h // 2 == d else []
                    leaving = (EZ1.at[d, s, u], base, TILES, unit) if s < 3 else None
                    items.append((slot, 2 * u + q, h, arrivals, leaving))
            if s < 3:
                sign_unit(EZ1.at[d, s, u], unit)
                relay(LR, 0, items)
                z1_copy(d, s + 1, u).start()
            else:
                UZ[slot] = unit
                relay(LR, 0, items)

    def z2_start():
        unit = UY[0]
        items = []
        for d in range(2):
            sign_unit(EZ20.at[d], unit)
            items += [(0, 3, 2 * d + e, [], (EZ20.at[d], e, 2, unit)) for e in range(2)]
        relay(TR, SPLIT, items)
        for d in range(2):
            z2_copy(d, 0).start()

    def z2_take(s):
        for d in range(2):
            z2_copy(d, s).wait_recv()
            ref = RZ20.at[d] if s == 0 else RZ21.at[d, s - 1]
            slot = CHAIN[d][s + 1]
            came = unit_of(ref)
            unit = jnp.maximum(UY[slot], came)
            items = []
            for h in range(TILES):
                arrivals = [(ref, h, TILES, came)]
                if s == 0:
                    arrivals = [(ref, h % 2, 2, came)] if h // 2 == d else []
                items.append((slot, 3, h, arrivals, (EZ21.at[d, s], h, TILES, unit) if s < 3 else None))
            if s < 3:
                sign_unit(EZ21.at[d, s], unit)
            relay(TR, SPLIT, items)
            if s < 3:
                z2_copy(d, s + 1).start()

    def y2_start():
        unit = UZ[7]
        items = []
        for d in range(2):
            sign_unit(EY20.at[d], unit)
            items += [(7, 0, 2 * d + e, [], (EY20.at[d], e, 2, unit)) for e in range(2)]
        relay(LR, 0, items)
        for d in range(2):
            y2_copy(d, 0).start()

    def y2_first():
        items = []
        for d in range(2):
            y2_copy(d, 0).wait_recv()
            came = unit_of(RY20.at[d])
            unit = jnp.maximum(UZ[7], came)
            sign_unit(EY21.at[d], unit)
            for h in range(TILES):
                arrivals = [(RY20.at[d], h % 2, 2, came)] if h // 2 == d else []
                items.append((7, QCHAIN[d][1], h, arrivals, (EY21.at[d], h, TILES, unit)))
        relay(LR, 0, items)
        for d in range(2):
            y2_copy(d, 1).start()

    def y2_last():
        items = []
        units = []
        for d in range(2):
            y2_copy(d, 1).wait_recv()
            units.append(unit_of(RY21.at[d]))
        for h in range(TILES):
            items.append((7, 3, h, [(RY21.at[d], h, TILES, units[d]) for d in range(2)], None))
        relay(LR, 0, items)

    FM[...] = jnp.zeros_like(FM)
    UT[...] = jnp.zeros_like(UT)
    UO[...] = jnp.zeros_like(UO)

    table = signs(False).astype(BF16)

    def turn(h):
        half_columns = pl.ds(h * 512, 512)
        pltpu.make_async_copy(
            g_ref.at[:, half_columns], gbuf.at[:, half_columns], g_sem.at[h]
        ).wait()
        for q in range(NY):
            start = h * 512 + q * BLOCK
            turned = lax.dot_general(
                table, gbuf[:, start : start + BLOCK], (((1,), (1,)), ((), ())),
                preferred_element_type=F32,
            )
            gt[start : start + BLOCK, :] = turned.astype(BF16)

    def finish(i):
        came = unit_of(CR.at[i])
        unit = [None]
        tops = [FM[...]]

        def put(j, r, value):
            if unit[0] is None:
                unit[0] = jnp.maximum(UO[...], came)
            for t in range(HALF // 16):
                row = r + t * 16
                for h in range(TILES):
                    tile = value[t * 16 : (t + 1) * 16, h * BLOCK : (h + 1) * BLOCK]
                    tile = tile + CR[i, (j * TILES + h) * 8 + row // 16].astype(F32)
                    if j == 0 and row >= SPLIT:
                        inverse = unit[0][8 + h : 9 + h] * (1.0 / STEP)
                        code, size = coded(tile * inverse)
                        EY0[h // 2, i, (row - SPLIT) // 16 * 2 + h % 2] = code
                        tops[0] = jnp.maximum(tops[0], size)
                    else:
                        S[i, j, row : row + 16, h * BLOCK : (h + 1) * BLOCK] = tile

        rounded_halves(w1.at[i % (LAG + 1)], put, UO)
        FM[...] = tops[0]
        UC[i] = unit[0]
        UZ[i] = unit[0]
        for d in range(2):
            sign_unit(EY0.at[d, i], unit[0])

    def leave(i):
        for d in range(2):
            y1_copy(i, d, 0).start()

    def landed(i):
        pltpu.make_async_copy(a_ref.at[:, pl.ds(0, WIDE)], abuf.at[i], a_sem.at[i]).wait()

    def multiply_sent(i):
        w0[...] = jnp.dot(gt[0:512, :], abuf[i], preferred_element_type=F32)

    def multiply_kept(i):
        w1[i % (LAG + 1)] = jnp.dot(gt[512:1024, :], abuf[i], preferred_element_type=F32)

    def round_sent(i):
        def put(j, r, value):
            for h in range(TILES):
                for t in range(HALF // 16):
                    tile = value[t * 16 : (t + 1) * 16, h * BLOCK : (h + 1) * BLOCK]
                    CS[i, (j * TILES + h) * 8 + r // 16 + t] = tile.astype(BF16)

        rounded_halves(w0, put, UT)
        CS[i, NY * TILES * 8] = UT[...].astype(BF16)

    def step(i, carry):
        landed(i)
        sib_copy(i - LAG).wait_recv()
        multiply_sent(i)
        finish(i - LAG)
        leave(i - LAG)

        @pl.when(i == LAG)
        def _():
            z1_start()

        @pl.when(i >= LAG + 2)
        def _():
            y1_first(i - LAG - 2)

        @pl.when(i == LAG + 2)
        def _():
            for u in range(2):
                z1_take(0, u)

        @pl.when(i == 7)
        def _():
            z1_take(1, 0)

        multiply_kept(i)
        round_sent(i)
        sib_copy(i).start()
        return carry

    turn(0)
    for q in range(NY):
        g_copy(1, q).start()
    lax.fori_loop(1, 8, start_a, 0)
    landed(0)
    multiply_sent(0)
    round_sent(0)
    pl.semaphore_wait(barrier, len(friends))
    sib_copy(0).start()
    turn(1)
    multiply_kept(0)
    for i in range(1, LAG):
        landed(i)
        multiply_sent(i)
        round_sent(i)
        sib_copy(i).start()
        multiply_kept(i)
    lax.fori_loop(LAG, 8, step, 0)
    def late(i):
        sib_copy(i).wait_recv()
        finish(i)
        leave(i)

    z1_take(1, 1)
    y1_last(0)
    z2_start()
    y1_first(3)
    late(5)
    y1_last(1)
    late(6)
    y1_first(4)
    y1_last(2)
    z1_take(2, 0)
    late(7)
    z2_take(0)
    y1_first(5)
    y1_last(3)
    z1_take(2, 1)
    y1_first(6)
    y1_last(4)
    z2_take(1)
    y1_first(7)
    z1_take(3, 0)
    y1_last(5)
    z1_take(3, 1)
    y2_start()
    y1_last(6)
    z2_take(2)
    y1_last(7)
    y2_first()
    FC[...] = FM[...]
    for d in range(1, 8):
        f_copy(d).start()
    z2_take(3)
    y2_last()

    part = S[7, 3]
    scale, inverse = scale_pair(jnp.max(jnp.abs(part), axis=0, keepdims=True), 31)
    value = jnp.floor(part * inverse + 0.5) * scale
    top = FM[...]
    remote(FR.at[pl.ds(1, 7)], FR.at[pl.ds(1, 7)], out_sem.at[9], f_r, sibling).wait_recv()
    for d in range(1, 8):
        top = jnp.maximum(top, FR[d])
    bad = jnp.where(top <= 2 * SPAN, 0.0, 1.0).astype(BF16)
    for r in (2, 1, 3, 0):
        turned = value[:, r * BLOCK : (r + 1) * BLOCK].T.astype(BF16)
        for g in range(8):
            XC[r * 8 + g, 0:16] = turned[g * 16 : (g + 1) * 16]
            XC[r * 8 + g, 16:32] = bad
        for p, d in peers:
            if p == r:
                x_copy(r, d).start()
    XR[0] = XC[place]

    gone = (CS, EY0, EY1, EZ0, EZ1, EZ20, EZ21, EY20, EY21, FR.at[pl.ds(1, 7)])
    for n, ref in enumerate(gone):
        remote(ref, ref, out_sem.at[n], x_r, sibling).wait_send()

    remaining = pl.ds(1, TILES * 8 - 1)
    remote(XR.at[remaining], XR.at[remaining], out_sem.at[10], x_r, sibling).wait_recv()
    total = XR[0:8, 0:16].astype(F32)
    for r in range(1, TILES):
        total = total + XR[r * 8 : r * 8 + 8, 0:16].astype(F32)
    flags = XR[:, 16:32].astype(F32).reshape(TILES * 8 * 16, BLOCK)
    bad_ref[...] = jnp.full_like(bad_ref, jnp.max(flags))
    result = jnp.dot(
        total.reshape(BLOCK, BLOCK), signs(True),
        preferred_element_type=F32, precision=lax.Precision.HIGHEST,
    ) * factor
    for d in range(8):
        columns = pl.ds(pl.multiple_of(((place + 8 - d) % 8) * BLOCK, BLOCK), BLOCK)
        out_ref[:, columns] = result[d * 16 : (d + 1) * 16]
    remote(XR.at[remaining], XR.at[remaining], out_sem.at[10], x_r, sibling).wait_send()


def quick(inputs, out_grads):
    tokens, din = inputs.shape
    width = out_grads.shape[1]
    everyone = lax.axis_size("hst") * lax.axis_size("chip")
    factor = 1.0 / (512.0 * math.sqrt(tokens * everyone))
    tall, low = TALL // 16 * TILES, SPLIT // 16 * TILES
    dma = pltpu.SemaphoreType.DMA

    def tiles(*shape):
        return [pltpu.VMEM(shape + (16, BLOCK), BF16)]

    def both(*shape):
        return tiles(*shape) * 2

    unit = pltpu.VMEM((8, 16, BLOCK), F32)
    return pl.pallas_call(
        functools.partial(kernel, factor),
        out_shape=(
            jax.ShapeDtypeStruct((din // everyone, width), F32),
            jax.ShapeDtypeStruct((8, BLOCK), F32),
        ),
        in_specs=[pl.BlockSpec(memory_space=pl.ANY)] * 2,
        out_specs=[pl.BlockSpec(memory_space=pltpu.VMEM)] * 2,
        scratch_shapes=[
            pltpu.VMEM((8, tokens, WIDE), BF16),
            pltpu.VMEM((tokens, width), BF16),
            pltpu.VMEM((width, tokens), BF16),
            pltpu.VMEM((512, WIDE), F32),
            pltpu.VMEM((LAG + 1, 512, WIDE), F32),
            pltpu.VMEM((8, NY, BLOCK, WIDE), F32),
        ]
        + both(8, NY * TILES * 8 + 1)
        + both(2, 8, tall // 2 + 1)
        + both(2, 8, tall + 1)
        + both(2, 2, low + 1)
        + both(2, 3, 2, 2 * low + 1)
        + both(2, tall // 2 + 1)
        + both(2, 3, tall + 1)
        + both(2, low // 2 + 1)
        + both(2, low + 1)
        + [
            pltpu.VMEM((TILES * 8, 32, BLOCK), BF16),
            pltpu.VMEM((TILES * 8, 32, BLOCK), BF16),
            pltpu.VMEM((16, BLOCK), F32),
            pltpu.VMEM((8, 16, BLOCK), F32),
            pltpu.VMEM((16, BLOCK), F32),
            pltpu.VMEM((16, BLOCK), F32),
            unit,
            unit,
            unit,
            pltpu.VMEM((16, BLOCK), F32),
        ]
        + [dma((8,)), dma((2,)), dma((8,)), dma((2, 2, 8)), dma((2, 4, 2)), dma((2, 4)), dma((2, 2))]
        + [dma, dma, dma((11,))],
        compiler_params=pltpu.CompilerParams(
            collective_id=0, has_side_effects=True, vmem_limit_bytes=60 * 2**20
        ),
        name="reduce_gradient",
    )(inputs, out_grads)


powers_list = [2.0**k for k in range(31)]
doubled_list = [2.0 ** (k + 1) for k in range(31)]


def hadamard_table(length):
    index = jnp.arange(length, dtype=jnp.int32)
    common = jnp.bitwise_and(index[:, None], index[None, :])
    parity = jnp.zeros((length, length), jnp.int32)
    for bit_number in range(length.bit_length() - 1):
        parity = parity + jnp.bitwise_and(jnp.right_shift(common, bit_number), 1)
    return 1.0 - 2.0 * (parity % 2).astype(jnp.float32)


def block_scale(largest):
    powers = jnp.array(powers_list, dtype=jnp.float32)
    doubled = jnp.array(doubled_list, dtype=jnp.float32)
    picked = jnp.where(largest[..., None] >= powers, doubled, jnp.ones_like(doubled))
    return jnp.max(picked, axis=-1) / 128.0


def quantize_last(values):
    scales = block_scale(jnp.max(jnp.abs(values), axis=-1))
    codes = jnp.floor(values / scales[..., None] + 0.5).astype(jnp.bfloat16)
    return (codes, scales)


def dequantize_last(codes, scales):
    return codes.astype(jnp.float32) * scales[..., None]


def plain(inputs, out_grads):
    table = hadamard_table(BLOCK)
    hosts = lax.axis_size("hst")
    chips = lax.axis_size("chip")
    din = inputs.shape[1]
    width = out_grads.shape[1]
    blocks = width // BLOCK
    rows = din // (hosts * chips)
    token_count = inputs.shape[0] * hosts * chips
    local = lax.dot_general(
        inputs, out_grads, (((0,), (0,)), ((), ())), preferred_element_type=jnp.float32
    )
    rotated = jnp.einsum(
        "dbj,jk->dbk", local.reshape(din, blocks, BLOCK), table, precision=lax.Precision.HIGHEST
    )
    codes, scales = quantize_last(rotated)
    codes = codes.reshape(hosts, chips, rows, width)
    scales = scales.reshape(hosts, chips, rows, blocks)
    got_codes, got_scales = (
        lax.all_to_all(codes, "chip", split_axis=1, concat_axis=1, tiled=True),
        lax.all_to_all(
            scales.astype(jnp.bfloat16), "chip", split_axis=1, concat_axis=1, tiled=True
        ).astype(scales.dtype),
    )
    count = got_codes.shape[0]
    shaped = got_codes.reshape(count, chips, rows, blocks, BLOCK)
    partial_value = jnp.sum(dequantize_last(shaped, got_scales), axis=1)
    count = partial_value.shape[0]
    new_codes, new_scales = quantize_last(partial_value)
    codes2 = new_codes.reshape(count, rows, width)
    own_codes, own_scales = (
        lax.all_to_all(codes2, "hst", split_axis=0, concat_axis=0, tiled=True),
        lax.all_to_all(
            new_scales.astype(jnp.bfloat16), "hst", split_axis=0, concat_axis=0, tiled=True
        ).astype(new_scales.dtype),
    )
    shaped = own_codes.reshape(hosts, rows, blocks, BLOCK)
    total = jnp.sum(dequantize_last(shaped, own_scales), axis=0)
    result = jnp.einsum("rbj,jk->rbk", total, table, precision=lax.Precision.HIGHEST)
    factor = 1.0 / (512.0 * jnp.sqrt(jnp.float32(token_count)))
    return result.reshape(rows, width) * factor


def body(inputs, out_grads):
    result, bad = quick(inputs, out_grads)
    return lax.cond(bad[0, 0] > 0, plain, lambda a, b: result, inputs, out_grads)


def solution(mesh):
    placed = (P(("hst", "chip"), None), P(("hst", "chip"), None))
    return jax.shard_map(
        body, mesh=mesh, in_specs=placed, out_specs=P(("hst", "chip"), None), check_vma=False
    )
```

```python
import functools
import math

import jax
import jax.numpy as jnp
from jax import lax
from jax.experimental import pallas as pl
from jax.experimental.pallas import tpu as pltpu
from jax.sharding import PartitionSpec as P

MESH = pl.DeviceIdType.MESH
F32 = jnp.float32
BF16 = jnp.bfloat16
BLOCK = 128
HALF = BLOCK // 2
NX, NZ, NY, NK = 4, 8, 4, 2
TILES = NX
WIDE = TILES * BLOCK
SPLIT = 48
TALL = BLOCK - SPLIT
CHAIN = ((0, 1, 3, 5, 7), (0, 2, 4, 6, 7))
LAG = 3
QCHAIN = ((0, 1, 3), (0, 2, 3))


STEP = 80.0
SPAN = 120.0
FAR = 2.0**22


def coded(number):
    size = jnp.abs(number)
    value = jnp.exp2(size - SPAN)
    return jnp.where(number < 0, -value, value).astype(BF16), size


def decoded(code, minus_unit):
    value = code.astype(F32)
    size = jnp.floor(jnp.log(jnp.abs(value)) * (STEP / math.log(2.0)) + (SPAN * STEP + 0.5))
    return size * jnp.where(value < 0, minus_unit, -minus_unit)


def signs(upper):
    i = lax.broadcasted_iota(jnp.int32, (BLOCK, BLOCK), 0)
    j = lax.broadcasted_iota(jnp.int32, (BLOCK, BLOCK), 1)
    t = i & j
    if not upper:
        t = t & (HALF - 1)
    t = t ^ (t >> 4)
    t = t ^ (t >> 2)
    t = t ^ (t >> 1)
    value = (1 - 2 * (t & 1)).astype(F32)
    if not upper:
        value = jnp.where((i & HALF) == (j & HALF), value, 0.0)
    return value


def scale_pair(largest, count):
    scale = jnp.full_like(largest, 1.0 / 128.0)
    inverse = jnp.full_like(largest, 128.0)
    for k in range(count):
        above = largest >= 2.0**k
        scale = jnp.where(above, 2.0 ** (k + 1) / 128.0, scale)
        inverse = jnp.where(above, 128.0 / 2.0 ** (k + 1), inverse)
    return scale, inverse


def rounded_halves(w_ref, put, units):
    tops = []
    for j in range(NY):
        u = w_ref[j * BLOCK : j * BLOCK + HALF]
        v = w_ref[j * BLOCK + HALF : (j + 1) * BLOCK]
        tops.append(jnp.max(jnp.abs(u) + jnp.abs(v), axis=0, keepdims=True))
    largest = jnp.concatenate(tops, axis=0)
    scale, inverse = scale_pair(largest, 22)
    used = largest >= 1.0
    minus = jnp.max(jnp.where(used, -scale, -FAR), axis=0, keepdims=True)
    finest = jnp.max(jnp.where(used, inverse, 1.0 / FAR), axis=0, keepdims=True)
    for h in range(TILES):
        units[h : h + 1, :] = minus[:, h * BLOCK : (h + 1) * BLOCK]
        units[8 + h : 9 + h, :] = finest[:, h * BLOCK : (h + 1) * BLOCK]
    for j in range(NY):
        s, inv = scale[j : j + 1], inverse[j : j + 1]
        u = w_ref[j * BLOCK : j * BLOCK + HALF] * inv
        v = w_ref[j * BLOCK + HALF : (j + 1) * BLOCK] * inv
        put(j, 0, jnp.floor(u + v + 0.5) * s)
        put(j, HALF, jnp.floor(u - v + 0.5) * s)


def kernel(
    factor, a_ref, g_ref, out_ref, bad_ref,
    abuf, gbuf, gt, w0, w1, S, CS, CR, EY0, RY0, EY1, RY1, EZ0, RZ0, EZ1, RZ1, EZ20, RZ20, EZ21, RZ21,
    EY20, RY20, EY21, RY21, XC, XR, FC, FR, UO, UT, UC, UY, UZ, FM,
    a_sem, g_sem, sib_r, y1_r, z1_r, z2_r, y2_r, x_r, f_r, out_sem,
):
    x = lax.axis_index("hst")
    c = lax.axis_index("chip")
    z, y, k = c // 8, (c // 2) % 4, c % 2

    def dev(x_, z_, y_, k_):
        return (x_, (z_ * NY + y_) * NK + k_)

    sibling = dev(x, z, y, 1 - k)
    y_next = (dev(x, z, (y + 1) % 4, k), dev(x, z, (y + 3) % 4, k))
    z_next = (dev(x, (z + 1) % 8, y, k), dev(x, (z + 7) % 8, y, k))
    place = y * 2 + k

    def owner(r, d):
        return ((x + r) % 4, z * 8 + (place + d) % 8)

    def along(d):
        return (x, ((z + d) % 8) * 8 + place)

    peers = [(r, d) for r in range(TILES) for d in range(8) if (r, d) != (0, 0)]
    peers.sort(key=lambda p: -2 * min(p[0], TILES - p[0]) - min(p[1], 8 - p[1]))

    def kv_columns(h, q):
        block = ((y + (2, 1, 3, 0)[q]) % 4) * 2 + (1 - k if h == 0 else k)
        return pl.ds(pl.multiple_of(block * BLOCK, BLOCK), BLOCK)

    def g_copy(h, q):
        start = h * 512 + q * BLOCK
        return pltpu.make_async_copy(
            g_ref.at[:, kv_columns(h, q)], gbuf.at[:, pl.ds(start, BLOCK)], g_sem.at[h]
        )

    def a_copy(i, r):
        off = jnp.where(i % 2 == 0, 4 + i // 2, 3 - i // 2)
        start = (((x + r) % 4) * 8 + (z + off) % 8) * BLOCK
        return pltpu.make_async_copy(
            a_ref.at[:, pl.ds(pl.multiple_of(start, BLOCK), BLOCK)],
            abuf.at[i, :, pl.ds(r * BLOCK, BLOCK)],
            a_sem.at[i],
        )

    def start_a(i, carry):
        for r in range(TILES):
            a_copy(i, r).start()
        return carry

    for q in range(NY):
        g_copy(0, q).start()
    start_a(0, 0)

    barrier = pltpu.get_barrier_semaphore()
    friends = [along(d) for d in range(1, 8)] + [owner(r, d) for r, d in peers]
    for friend in friends:
        pl.semaphore_signal(barrier, inc=1, device_id=friend, device_id_type=MESH)

    def remote(src, dst, ss, rs, to):
        return pltpu.make_async_remote_copy(
            src_ref=src, dst_ref=dst, send_sem=ss, recv_sem=rs, device_id=to, device_id_type=MESH
        )

    def sib_copy(i):
        return remote(CS.at[i], CR.at[i], out_sem.at[0], sib_r.at[i], sibling)

    def sib_start(i):
        for part, size in ((0, 33), (33, 32), (65, 32), (97, 32)):
            tiles = pl.ds(part, size)
            remote(CS.at[i, tiles], CR.at[i, tiles], out_sem.at[0], sib_r.at[i], sibling).start()

    def y1_copy(i, d, s):
        src, dst = (EY0, RY0) if s == 0 else (EY1, RY1)
        return remote(src.at[d, i], dst.at[d, i], out_sem.at[1 + s], y1_r.at[d, s, i], y_next[d])

    def z1_copy(d, s, u):
        if s == 0:
            src, dst = EZ0.at[d, u], RZ0.at[d, u]
        else:
            src, dst = EZ1.at[d, s - 1, u], RZ1.at[d, s - 1, u]
        return remote(src, dst, out_sem.at[3 + min(s, 1)], z1_r.at[d, s, u], z_next[d])

    def z2_copy(d, s):
        if s == 0:
            src, dst = EZ20.at[d], RZ20.at[d]
        else:
            src, dst = EZ21.at[d, s - 1], RZ21.at[d, s - 1]
        return remote(src, dst, out_sem.at[5 + min(s, 1)], z2_r.at[d, s], z_next[d])

    def y2_copy(d, s):
        src, dst = (EY20, RY20) if s == 0 else (EY21, RY21)
        return remote(src.at[d], dst.at[d], out_sem.at[7 + s], y2_r.at[d, s], y_next[d])

    def f_copy(d):
        return remote(FC, FR.at[d], out_sem.at[9], f_r, along(d))

    def x_copy(r, d):
        src = XC.at[r * 8 + (place + d) % 8]
        return remote(src, XR.at[r * 8 + d], out_sem.at[10], x_r, owner(r, d))

    def relay(count, row, items):
        def one(t, top):
            rows = pl.ds(pl.multiple_of(row + 16 * t, 16), 16)
            for i, q, h, arrivals, leaving in items:
                columns = slice(h * BLOCK, (h + 1) * BLOCK)
                v = S[i, q, rows, columns]
                for ref, base, stride, unit in arrivals:
                    v = v + decoded(ref[base + stride * t], unit[h : h + 1])
                if leaving is None:
                    S[i, q, rows, columns] = v
                else:
                    ref, base, stride, unit = leaving
                    code, size = coded(v * (unit[8 + h : 9 + h] * (1.0 / STEP)))
                    ref[base + stride * t] = code
                    top = jnp.maximum(top, size)
            return top

        FM[...] = lax.fori_loop(0, count, one, FM[...], unroll=True)

    TR, LR = TALL // 16, SPLIT // 16

    def unit_of(ref):
        return ref[ref.shape[0] - 1].astype(F32)

    def sign_unit(ref, unit):
        ref[ref.shape[0] - 1] = unit.astype(BF16)

    def y1_first(i):
        items = []
        for d in range(2):
            y1_copy(i, d, 0).wait_recv()
            came = unit_of(RY0.at[d, i])
            unit = jnp.maximum(UC[i], came)
            sign_unit(EY1.at[d, i], unit)
            for h in range(TILES):
                arrivals = [(RY0.at[d, i], h % 2, 2, came)] if h // 2 == d else []
                items.append((i, QCHAIN[d][1], h, arrivals, (EY1.at[d, i], h, TILES, unit)))
        relay(TR, SPLIT, items)
        for d in range(2):
            y1_copy(i, d, 1).start()

    def y1_last(i):
        units = []
        for d in range(2):
            y1_copy(i, d, 1).wait_recv()
            units.append(unit_of(RY1.at[d, i]))
        arrivals = [[(RY1.at[d, i], h, TILES, units[d]) for d in range(2)] for h in range(TILES)]
        relay(TR, SPLIT, [(i, 3, h, arrivals[h], None) for h in range(TILES)])
        UY[i] = jnp.maximum(UC[i], jnp.maximum(units[0], units[1]))

    def z1_start():
        unit = UC[0]
        for u in range(2):
            items = []
            for d in range(2):
                sign_unit(EZ0.at[d, u], unit)
                for q in range(2):
                    for e in range(2):
                        leaving = (EZ0.at[d, u], q * LR * 2 + e, 2, unit)
                        items.append((0, 2 * u + q, 2 * d + e, [], leaving))
            relay(LR, 0, items)
            for d in range(2):
                z1_copy(d, 0, u).start()

    def z1_take(s, u):
        for d in range(2):
            z1_copy(d, s, u).wait_recv()
            ref = RZ0.at[d, u] if s == 0 else RZ1.at[d, s - 1, u]
            slot = CHAIN[d][s + 1]
            came = unit_of(ref)
            unit = jnp.maximum(UZ[slot], came)
            items = []
            for q in range(2):
                for h in range(TILES):
                    base = q * LR * TILES + h
                    arrivals = [(ref, base, TILES, came)]
                    if s == 0:
                        arrivals = [(ref, q * LR * 2 + h % 2, 2, came)] if h // 2 == d else []
                    leaving = (EZ1.at[d, s, u], base, TILES, unit) if s < 3 else None
                    items.append((slot, 2 * u + q, h, arrivals, leaving))
            if s < 3:
                sign_unit(EZ1.at[d, s, u], unit)
                relay(LR, 0, items)
                z1_copy(d, s + 1, u).start()
            else:
                UZ[slot] = unit
                relay(LR, 0, items)

    def z2_start():
        unit = UY[0]
        items = []
        for d in range(2):
            sign_unit(EZ20.at[d], unit)
            items += [(0, 3, 2 * d + e, [], (EZ20.at[d], e, 2, unit)) for e in range(2)]
        relay(TR, SPLIT, items)
        for d in range(2):
            z2_copy(d, 0).start()

    def z2_take(s):
        for d in range(2):
            z2_copy(d, s).wait_recv()
            ref = RZ20.at[d] if s == 0 else RZ21.at[d, s - 1]
            slot = CHAIN[d][s + 1]
            came = unit_of(ref)
            unit = jnp.maximum(UY[slot], came)
            items = []
            for h in range(TILES):
                arrivals = [(ref, h, TILES, came)]
                if s == 0:
                    arrivals = [(ref, h % 2, 2, came)] if h // 2 == d else []
                items.append((slot, 3, h, arrivals, (EZ21.at[d, s], h, TILES, unit) if s < 3 else None))
            if s < 3:
                sign_unit(EZ21.at[d, s], unit)
            relay(TR, SPLIT, items)
            if s < 3:
                z2_copy(d, s + 1).start()

    def y2_start():
        unit = UZ[7]
        items = []
        for d in range(2):
            sign_unit(EY20.at[d], unit)
            items += [(7, 0, 2 * d + e, [], (EY20.at[d], e, 2, unit)) for e in range(2)]
        relay(LR, 0, items)
        for d in range(2):
            y2_copy(d, 0).start()

    def y2_first():
        items = []
        for d in range(2):
            y2_copy(d, 0).wait_recv()
            came = unit_of(RY20.at[d])
            unit = jnp.maximum(UZ[7], came)
            sign_unit(EY21.at[d], unit)
            for h in range(TILES):
                arrivals = [(RY20.at[d], h % 2, 2, came)] if h // 2 == d else []
                items.append((7, QCHAIN[d][1], h, arrivals, (EY21.at[d], h, TILES, unit)))
        relay(LR, 0, items)
        for d in range(2):
            y2_copy(d, 1).start()

    def y2_last():
        items = []
        units = []
        for d in range(2):
            y2_copy(d, 1).wait_recv()
            units.append(unit_of(RY21.at[d]))
        for h in range(TILES):
            items.append((7, 3, h, [(RY21.at[d], h, TILES, units[d]) for d in range(2)], None))
        relay(LR, 0, items)

    FM[...] = jnp.zeros_like(FM)
    UT[...] = jnp.zeros_like(UT)
    UO[...] = jnp.zeros_like(UO)

    table = signs(False).astype(BF16)

    def turn(h):
        half_columns = pl.ds(h * 512, 512)
        pltpu.make_async_copy(
            g_ref.at[:, half_columns], gbuf.at[:, half_columns], g_sem.at[h]
        ).wait()
        for q in range(NY):
            start = h * 512 + q * BLOCK
            turned = lax.dot_general(
                table, gbuf[:, start : start + BLOCK], (((1,), (1,)), ((), ())),
                preferred_element_type=F32,
            )
            gt[start : start + BLOCK, :] = turned.astype(BF16)

    def finish(i):
        came = unit_of(CR.at[i])
        unit = [None]
        tops = [FM[...]]

        def put(j, r, value):
            if unit[0] is None:
                unit[0] = jnp.maximum(UO[...], came)
            for t in range(HALF // 16):
                row = r + t * 16
                for h in range(TILES):
                    tile = value[t * 16 : (t + 1) * 16, h * BLOCK : (h + 1) * BLOCK]
                    tile = tile + CR[i, (j * TILES + h) * 8 + row // 16].astype(F32)
                    if j == 0 and row >= SPLIT:
                        inverse = unit[0][8 + h : 9 + h] * (1.0 / STEP)
                        code, size = coded(tile * inverse)
                        EY0[h // 2, i, (row - SPLIT) // 16 * 2 + h % 2] = code
                        tops[0] = jnp.maximum(tops[0], size)
                    else:
                        S[i, j, row : row + 16, h * BLOCK : (h + 1) * BLOCK] = tile

        rounded_halves(w1.at[i % (LAG + 1)], put, UO)
        FM[...] = tops[0]
        UC[i] = unit[0]
        UZ[i] = unit[0]
        for d in range(2):
            sign_unit(EY0.at[d, i], unit[0])

    def leave(i):
        for d in range(2):
            y1_copy(i, d, 0).start()

    def landed(i):
        pltpu.make_async_copy(a_ref.at[:, pl.ds(0, WIDE)], abuf.at[i], a_sem.at[i]).wait()

    def multiply_sent(i):
        w0[...] = jnp.dot(gt[0:512, :], abuf[i], preferred_element_type=F32)

    def multiply_kept(i):
        w1[i % (LAG + 1)] = jnp.dot(gt[512:1024, :], abuf[i], preferred_element_type=F32)

    def round_sent(i):
        def put(j, r, value):
            for h in range(TILES):
                for t in range(HALF // 16):
                    tile = value[t * 16 : (t + 1) * 16, h * BLOCK : (h + 1) * BLOCK]
                    CS[i, (j * TILES + h) * 8 + r // 16 + t] = tile.astype(BF16)

        rounded_halves(w0, put, UT)
        CS[i, NY * TILES * 8] = UT[...].astype(BF16)

    def step(i, carry):
        landed(i)
        sib_copy(i - LAG).wait_recv()
        multiply_sent(i)
        finish(i - LAG)
        leave(i - LAG)

        @pl.when(i == LAG)
        def _():
            z1_start()

        @pl.when(i >= LAG + 2)
        def _():
            y1_first(i - LAG - 2)

        @pl.when(i == LAG + 2)
        def _():
            for u in range(2):
                z1_take(0, u)

        @pl.when(i == 7)
        def _():
            z1_take(1, 0)

        multiply_kept(i)
        round_sent(i)
        sib_start(i)
        return carry

    turn(0)
    for q in range(NY):
        g_copy(1, q).start()
    lax.fori_loop(1, 8, start_a, 0)
    landed(0)
    multiply_sent(0)
    round_sent(0)
    pl.semaphore_wait(barrier, len(friends))
    sib_start(0)
    turn(1)
    multiply_kept(0)
    for i in range(1, LAG):
        landed(i)
        multiply_sent(i)
        round_sent(i)
        sib_start(i)
        multiply_kept(i)
    lax.fori_loop(LAG, 8, step, 0)
    def late(i):
        sib_copy(i).wait_recv()
        finish(i)
        leave(i)

    z1_take(1, 1)
    y1_last(0)
    z2_start()
    y1_first(3)
    late(5)
    y1_last(1)
    late(6)
    y1_first(4)
    y1_last(2)
    z1_take(2, 0)
    late(7)
    z2_take(0)
    y1_first(5)
    y1_last(3)
    z1_take(2, 1)
    y1_first(6)
    y1_last(4)
    z2_take(1)
    y1_first(7)
    z1_take(3, 0)
    y1_last(5)
    z1_take(3, 1)
    y2_start()
    y1_last(6)
    z2_take(2)
    y1_last(7)
    y2_first()
    FC[...] = FM[...]
    for d in range(1, 8):
        f_copy(d).start()
    z2_take(3)
    y2_last()

    part = S[7, 3]
    scale, inverse = scale_pair(jnp.max(jnp.abs(part), axis=0, keepdims=True), 31)
    value = jnp.floor(part * inverse + 0.5) * scale
    top = FM[...]
    remote(FR.at[pl.ds(1, 7)], FR.at[pl.ds(1, 7)], out_sem.at[9], f_r, sibling).wait_recv()
    for d in range(1, 8):
        top = jnp.maximum(top, FR[d])
    bad = jnp.where(top <= 2 * SPAN, 0.0, 1.0).astype(BF16)
    for r in (2, 1, 3, 0):
        turned = value[:, r * BLOCK : (r + 1) * BLOCK].T.astype(BF16)
        for g in range(8):
            XC[r * 8 + g, 0:16] = turned[g * 16 : (g + 1) * 16]
            XC[r * 8 + g, 16:32] = bad
        for p, d in peers:
            if p == r:
                x_copy(r, d).start()
    XR[0] = XC[place]

    gone = (CS, EY0, EY1, EZ0, EZ1, EZ20, EZ21, EY20, EY21, FR.at[pl.ds(1, 7)])
    for n, ref in enumerate(gone):
        remote(ref, ref, out_sem.at[n], x_r, sibling).wait_send()

    remaining = pl.ds(1, TILES * 8 - 1)
    remote(XR.at[remaining], XR.at[remaining], out_sem.at[10], x_r, sibling).wait_recv()
    total = XR[0:8, 0:16].astype(F32)
    for r in range(1, TILES):
        total = total + XR[r * 8 : r * 8 + 8, 0:16].astype(F32)
    flags = XR[:, 16:32].astype(F32).reshape(TILES * 8 * 16, BLOCK)
    bad_ref[...] = jnp.full_like(bad_ref, jnp.max(flags))
    result = jnp.dot(
        total.reshape(BLOCK, BLOCK), signs(True),
        preferred_element_type=F32, precision=lax.Precision.HIGHEST,
    ) * factor
    for d in range(8):
        columns = pl.ds(pl.multiple_of(((place + 8 - d) % 8) * BLOCK, BLOCK), BLOCK)
        out_ref[:, columns] = result[d * 16 : (d + 1) * 16]
    remote(XR.at[remaining], XR.at[remaining], out_sem.at[10], x_r, sibling).wait_send()


def quick(inputs, out_grads):
    tokens, din = inputs.shape
    width = out_grads.shape[1]
    everyone = lax.axis_size("hst") * lax.axis_size("chip")
    factor = 1.0 / (512.0 * math.sqrt(tokens * everyone))
    tall, low = TALL // 16 * TILES, SPLIT // 16 * TILES
    dma = pltpu.SemaphoreType.DMA

    def tiles(*shape):
        return [pltpu.VMEM(shape + (16, BLOCK), BF16)]

    def both(*shape):
        return tiles(*shape) * 2

    unit = pltpu.VMEM((8, 16, BLOCK), F32)
    return pl.pallas_call(
        functools.partial(kernel, factor),
        out_shape=(
            jax.ShapeDtypeStruct((din // everyone, width), F32),
            jax.ShapeDtypeStruct((8, BLOCK), F32),
        ),
        in_specs=[pl.BlockSpec(memory_space=pl.ANY)] * 2,
        out_specs=[pl.BlockSpec(memory_space=pltpu.VMEM)] * 2,
        scratch_shapes=[
            pltpu.VMEM((8, tokens, WIDE), BF16),
            pltpu.VMEM((tokens, width), BF16),
            pltpu.VMEM((width, tokens), BF16),
            pltpu.VMEM((512, WIDE), F32),
            pltpu.VMEM((LAG + 1, 512, WIDE), F32),
            pltpu.VMEM((8, NY, BLOCK, WIDE), F32),
        ]
        + both(8, NY * TILES * 8 + 1)
        + both(2, 8, tall // 2 + 1)
        + both(2, 8, tall + 1)
        + both(2, 2, low + 1)
        + both(2, 3, 2, 2 * low + 1)
        + both(2, tall // 2 + 1)
        + both(2, 3, tall + 1)
        + both(2, low // 2 + 1)
        + both(2, low + 1)
        + [
            pltpu.VMEM((TILES * 8, 32, BLOCK), BF16),
            pltpu.VMEM((TILES * 8, 32, BLOCK), BF16),
            pltpu.VMEM((16, BLOCK), F32),
            pltpu.VMEM((8, 16, BLOCK), F32),
            pltpu.VMEM((16, BLOCK), F32),
            pltpu.VMEM((16, BLOCK), F32),
            unit,
            unit,
            unit,
            pltpu.VMEM((16, BLOCK), F32),
        ]
        + [dma((8,)), dma((2,)), dma((8,)), dma((2, 2, 8)), dma((2, 4, 2)), dma((2, 4)), dma((2, 2))]
        + [dma, dma, dma((11,))],
        compiler_params=pltpu.CompilerParams(
            collective_id=0, has_side_effects=True, vmem_limit_bytes=60 * 2**20
        ),
        name="reduce_gradient",
    )(inputs, out_grads)


powers_list = [2.0**k for k in range(31)]
doubled_list = [2.0 ** (k + 1) for k in range(31)]


def hadamard_table(length):
    index = jnp.arange(length, dtype=jnp.int32)
    common = jnp.bitwise_and(index[:, None], index[None, :])
    parity = jnp.zeros((length, length), jnp.int32)
    for bit_number in range(length.bit_length() - 1):
        parity = parity + jnp.bitwise_and(jnp.right_shift(common, bit_number), 1)
    return 1.0 - 2.0 * (parity % 2).astype(jnp.float32)


def block_scale(largest):
    powers = jnp.array(powers_list, dtype=jnp.float32)
    doubled = jnp.array(doubled_list, dtype=jnp.float32)
    picked = jnp.where(largest[..., None] >= powers, doubled, jnp.ones_like(doubled))
    return jnp.max(picked, axis=-1) / 128.0


def quantize_last(values):
    scales = block_scale(jnp.max(jnp.abs(values), axis=-1))
    codes = jnp.floor(values / scales[..., None] + 0.5).astype(jnp.bfloat16)
    return (codes, scales)


def dequantize_last(codes, scales):
    return codes.astype(jnp.float32) * scales[..., None]


def plain(inputs, out_grads):
    table = hadamard_table(BLOCK)
    hosts = lax.axis_size("hst")
    chips = lax.axis_size("chip")
    din = inputs.shape[1]
    width = out_grads.shape[1]
    blocks = width // BLOCK
    rows = din // (hosts * chips)
    token_count = inputs.shape[0] * hosts * chips
    local = lax.dot_general(
        inputs, out_grads, (((0,), (0,)), ((), ())), preferred_element_type=jnp.float32
    )
    rotated = jnp.einsum(
        "dbj,jk->dbk", local.reshape(din, blocks, BLOCK), table, precision=lax.Precision.HIGHEST
    )
    codes, scales = quantize_last(rotated)
    codes = codes.reshape(hosts, chips, rows, width)
    scales = scales.reshape(hosts, chips, rows, blocks)
    got_codes, got_scales = (
        lax.all_to_all(codes, "chip", split_axis=1, concat_axis=1, tiled=True),
        lax.all_to_all(
            scales.astype(jnp.bfloat16), "chip", split_axis=1, concat_axis=1, tiled=True
        ).astype(scales.dtype),
    )
    count = got_codes.shape[0]
    shaped = got_codes.reshape(count, chips, rows, blocks, BLOCK)
    partial_value = jnp.sum(dequantize_last(shaped, got_scales), axis=1)
    count = partial_value.shape[0]
    new_codes, new_scales = quantize_last(partial_value)
    codes2 = new_codes.reshape(count, rows, width)
    own_codes, own_scales = (
        lax.all_to_all(codes2, "hst", split_axis=0, concat_axis=0, tiled=True),
        lax.all_to_all(
            new_scales.astype(jnp.bfloat16), "hst", split_axis=0, concat_axis=0, tiled=True
        ).astype(new_scales.dtype),
    )
    shaped = own_codes.reshape(hosts, rows, blocks, BLOCK)
    total = jnp.sum(dequantize_last(shaped, own_scales), axis=0)
    result = jnp.einsum("rbj,jk->rbk", total, table, precision=lax.Precision.HIGHEST)
    factor = 1.0 / (512.0 * jnp.sqrt(jnp.float32(token_count)))
    return result.reshape(rows, width) * factor


def body(inputs, out_grads):
    result, bad = quick(inputs, out_grads)
    return lax.cond(bad[0, 0] > 0, plain, lambda a, b: result, inputs, out_grads)


def solution(mesh):
    placed = (P(("hst", "chip"), None), P(("hst", "chip"), None))
    return jax.shard_map(
        body, mesh=mesh, in_specs=placed, out_specs=P(("hst", "chip"), None), check_vma=False
    )
```
